256 devices in a mesh: frames: 4 (over y), rows: 64 (over x, z, core).
Axes of the slice: x: 4, y: 4, z: 8, core: 2. Of those that a mesh axis runs over, the one named last changes fastest.
Arguments:
- inputs: bfloat16 [4, 256, 424, 256], P('frames', 'rows'), may hold values from -350 to 350, as said below
- cotangent: bfloat16 [4, 256, 424, 256], P('frames', 'rows'), may hold values from -140 to 140, as said below
- kernel: bfloat16 [3, 3, 3, 256, 256], replicated, may hold values from -0.078125 to 0.078125
- norm_gain: float32 [256], replicated, may hold values from 0.1 to 1.9
- norm_bias: float32 [256], replicated, may hold values from -1 to 1
Outputs:
- input_grad: bfloat16 [4, 256, 424, 256], P('frames', 'rows')
The draws below stay inside these ranges and needn't reach their ends.
Inputs may be any that keep to these rules, and one draw needn't show every extreme that they name: `inputs`: finite values. `cotangent`: finite values.
All inputs are finite; a program needn't handle non-finite values.
Results may differ from the reference program's by a relative error of at most 0.0055.
Values may be sent and summed in bfloat16 or wider, within the bound.
A program may use at most 64 MiB of HBM per device.

```python
import math
import jax
import jax.numpy as jnp
from jax import lax

C = 256
GROUPS = 32
WIDTH = 424
HEIGHT = 256
FRAMES = 4


def frame_factors():
    steps = jnp.arange(FRAMES, dtype=jnp.float32)
    factor = (1.0 + 0.5 * steps) / (1.0 + 0.5 * (FRAMES - 1))
    shift = 1.5 * (2.0 * steps / max(FRAMES - 1, 1) - 1.0)
    return (factor, shift)


def draw_inputs(key, part):
    keys = jax.random.split(jax.random.fold_in(key, 11), 4)
    shape = (FRAMES, HEIGHT, WIDTH, C)
    rows = jnp.arange(HEIGHT, dtype=jnp.float32) / max(HEIGHT - 1, 1)
    chan_scale = jnp.exp(jax.random.uniform(keys[1], (C,), jnp.float32, 0.0, math.log(10.0)))
    col_scale = jnp.exp(jax.random.uniform(keys[2], (WIDTH,), jnp.float32, 0.0, math.log(3.0)))
    offset = jax.random.uniform(keys[3], (C,), jnp.float32, -2.0, 2.0)
    factor, shift = frame_factors()
    noise = jnp.clip(jax.random.normal(keys[0], shape, jnp.float32), -4.0, 4.0)
    row_scale = 3.0 ** rows
    spread = noise * row_scale[:, None, None] * col_scale[:, None] * factor[:, None, None, None]
    values = offset + (spread + shift[:, None, None, None]) * chan_scale / 3.0
    return values.astype(jnp.bfloat16)


def draw_cotangent(key, part):
    keys = jax.random.split(jax.random.fold_in(key, 23), 4)
    shape = (FRAMES, HEIGHT, WIDTH, C)
    rows = jnp.arange(HEIGHT, dtype=jnp.float32) / max(HEIGHT - 1, 1)
    chan_scale = jnp.exp(jax.random.uniform(keys[1], (C,), jnp.float32, 0.0, math.log(4.0)))
    col_scale = jnp.exp(jax.random.uniform(keys[2], (WIDTH,), jnp.float32, 0.0, math.log(3.0)))
    offset = jax.random.uniform(keys[3], (C,), jnp.float32, -1.0, 1.0)
    factor, shift = frame_factors()
    noise = jnp.clip(jax.random.normal(keys[0], shape, jnp.float32), -4.0, 4.0)
    row_scale = 3.0 ** rows
    values = offset + noise * row_scale[:, None, None] * col_scale[:, None] * chan_scale / 3.0
    values = values * factor[:, None, None, None]
    return values.astype(jnp.bfloat16)


def gaussian(own_key, shape, deviation, limit, held_as=jnp.bfloat16):
    result = jax.random.normal(own_key, shape, jnp.float32) * deviation
    return jnp.minimum(jnp.maximum(result, -limit), limit).astype(held_as)


def setup_inputs(seed: int = 0) -> dict:
    streams_of = jax.random.split(jax.random.key(seed), 6)
    return {
        "inputs": draw_inputs(jax.random.fold_in(streams_of[5], 71), 0),
        "cotangent": draw_cotangent(jax.random.fold_in(streams_of[5], 71), 0),
        "kernel": gaussian(streams_of[2], (3, 3, 3, C, C), (27 * C) ** -0.5, 0.078125),
        "norm_gain": jnp.clip(1.0 + 0.18 * jax.random.normal(streams_of[3], (C,), jnp.float32), 0.1, 1.9),
        "norm_bias": jnp.clip(jax.random.uniform(streams_of[4], (C,), jnp.float32, -1.0, 1.0), -1.0, 1.0),
    }


EPS = 1e-06

def group_sum(values):
    per_chan = lax.optimization_barrier(jnp.sum(values, axis=(0, 1, 2)))
    return lax.optimization_barrier(jnp.sum(per_chan.reshape(GROUPS, -1), axis=1))

def spread_groups(per_group, channels):
    return jnp.repeat(per_group, channels // GROUPS)

def reference(inputs, cotangent, kernel, norm_gain, norm_bias):
    values = inputs.astype(jnp.float32)
    channels = values.shape[-1]
    cells_per = values.shape[0] * values.shape[1] * values.shape[2] * (channels // GROUPS)
    centre = group_sum(values) / cells_per
    centred = values - spread_groups(centre, channels)
    variance = group_sum(centred * centred) / cells_per
    inv_std = spread_groups(lax.rsqrt(variance + EPS), channels)
    normed = centred * inv_std
    preact = normed * norm_gain + norm_bias
    weights = kernel.astype(jnp.float32)

    def forward(active):
        return lax.conv_general_dilated(active[None], weights, (1, 1, 1), ((2, 0), (1, 1), (1, 1)), dimension_numbers=('NDHWC', 'DHWIO', 'NDHWC'), precision=lax.Precision.HIGHEST)[0]
    _, pullback = jax.vjp(forward, jnp.zeros_like(values))
    act_grad = pullback(cotangent.astype(jnp.float32))[0]
    logistic = jax.nn.sigmoid(preact)
    norm_grad = act_grad * logistic * (1.0 + preact * (1.0 - logistic)) * norm_gain
    grad_total = group_sum(norm_grad) / cells_per
    grad_cross = group_sum(norm_grad * normed) / cells_per
    input_grad = inv_std * (norm_grad - spread_groups(grad_total, channels) - normed * spread_groups(grad_cross, channels))
    return input_grad.astype(jnp.bfloat16)
```

```python
import functools

import jax
import jax.numpy as jnp
from jax import lax
from jax.experimental import pallas as pl
from jax.experimental.pallas import tpu as pltpu
from jax.sharding import PartitionSpec as P

GROUPS = 32
EPS = 1e-06
MESH = pl.DeviceIdType.MESH
FRAMES, STRIPS = 4, 64
PAD = 8


def plane_peers(f, r):
    out = []
    for dy in range(4):
        for dx in range(4):
            if dy or dx:
                out.append((lax.rem(f + dy, 4), lax.rem(r + 16 * dx, 64)))
    return out


def line_peers(f, r):
    base, low = 16 * (r // 16), lax.rem(r, 16)
    return [(f, base + lax.rem(low + d, 16)) for d in range(1, 16)]


def over_group(total, channels):
    lane = lax.broadcasted_iota(jnp.int32, total.shape, 1)
    step = 1
    while step < channels // GROUPS:
        up = pltpu.roll(total, channels - step, 1)
        down = pltpu.roll(total, step, 1)
        total = total + jnp.where((lane // step) % 2 == 0, up, down)
        step *= 2
    return total


def body(
    cells_per, x_hbm, cot_hbm, k_hbm, gain_ref, bias_ref, g_ref, stat_ref,
    xin, cot, weights, acc, slope, cur, near, far,
    lsem, own_send, frame_recv, relay_send, halo_send, halo_recv, ar_send, ar_recv,
):
    f, r = lax.axis_index("frames"), lax.axis_index("rows")
    rows, width, channels = xin.shape
    half = channels // 2
    slots = 3 - (f // 2) * (f - 1)

    load_cot = pltpu.make_async_copy(cot_hbm.at[0], cot.at[0, pl.ds(1, rows)], lsem.at[0])
    load_x = pltpu.make_async_copy(x_hbm.at[0], xin, lsem.at[1])
    load_k = pltpu.make_async_copy(k_hbm, weights, lsem.at[2])
    load_cot.start()
    load_x.start()
    load_k.start()

    barrier = pltpu.get_barrier_semaphore()
    greeted = plane_peers(f, r) + line_peers(f, r)
    greeted += [(f, lax.rem(r + 1, STRIPS)), (f, lax.rem(r + STRIPS - 1, STRIPS))]
    for peer in greeted:
        pl.semaphore_signal(barrier, inc=1, device_id=peer, device_id_type=MESH)

    acc[...] = jnp.zeros_like(acc)
    load_x.wait()

    def add_stats(y, carry):
        values = xin[y].astype(jnp.float32)
        return (
            carry[0] + jnp.sum(values, axis=0, keepdims=True),
            carry[1] + jnp.sum(values * values, axis=0, keepdims=True),
        )

    zero = jnp.zeros((1, channels), jnp.float32)
    first, second = lax.fori_loop(0, rows, add_stats, (zero, zero))
    load_cot.wait()
    pl.semaphore_wait(barrier, len(greeted))

    def piece(slot, row, h):
        return cot.at[slot, row, :, pl.ds(h * half, half)]

    def own_copy(q, h):
        row, slot = 1 + lax.rem(3 * q, 4), 2 - lax.rem(f, 2)
        return pltpu.make_async_remote_copy(
            piece(0, row, h), piece(slot, row, h), own_send.at[q, h],
            frame_recv.at[slot - 1, q, h], device_id=((f // 3) * 2, r), device_id_type=MESH,
        )

    def relay_copy(q, h):
        row, source, slot = 1 + lax.rem(3 * q, 4), 2 - f // 2, 1 + f // 2
        return pltpu.make_async_remote_copy(
            piece(source, row, h), piece(slot, row, h), relay_send.at[q, h],
            frame_recv.at[slot - 1, q, h], device_id=(1, r), device_id_type=MESH,
        )

    def await_piece(slot, q, h):
        row = 1 + lax.rem(3 * q, 4)
        pltpu.make_async_remote_copy(
            piece(slot, row, h), piece(slot, row, h), own_send.at[q, h],
            frame_recv.at[slot - 1, q, h], device_id=(f, r), device_id_type=MESH,
        ).wait_recv()

    def halo_up(a):
        return pltpu.make_async_remote_copy(
            cot.at[a, 1], cot.at[a, rows + 1], halo_send.at[a, 0], halo_recv.at[a, 0],
            device_id=(f, lax.rem(r + STRIPS - 1, STRIPS)), device_id_type=MESH,
        )

    def halo_down(a):
        return pltpu.make_async_remote_copy(
            cot.at[a, rows], cot.at[a, 0], halo_send.at[a, 1], halo_recv.at[a, 1],
            device_id=(f, lax.rem(r + 1, STRIPS)), device_id_type=MESH,
        )

    @pl.when(f > 0)
    def _():
        for q in range(4):
            for h in range(2):
                own_copy(q, h).start()

    @pl.when(r > 0)
    def _():
        halo_up(0).start()

    @pl.when(r < STRIPS - 1)
    def _():
        halo_down(0).start()

    def send_stage(k, peers, slots_ref):
        for j, peer in enumerate(peers):
            pltpu.make_async_remote_copy(
                cur.at[k], slots_ref.at[j], ar_send.at[k], ar_recv.at[k],
                device_id=peer, device_id_type=MESH,
            ).start()

    def whole_stage(k, slots_ref):
        return pltpu.make_async_remote_copy(
            slots_ref, slots_ref, ar_send.at[k], ar_recv.at[k],
            device_id=(f, r), device_id_type=MESH,
        )

    def end_stage(k, slots_ref):
        whole_stage(k, slots_ref).wait_recv()
        return cur[k] + jnp.sum(slots_ref[...], axis=0)

    cur[0] = jnp.concatenate([first, second], axis=0)
    send_stage(0, plane_peers(f, r), near.at[0])

    def add_row(a, row):
        def tap(b, carry):
            y = row - b

            @pl.when((y >= 0) & (y < rows))
            def _():
                acc[y, pl.ds(PAD, width), :] += lax.dot_general(
                    cot[a, row], weights[2 - a, 2 - b], (((1,), (1,)), ((), ())),
                    preferred_element_type=jnp.float32,
                )
            return carry

        lax.fori_loop(0, 3, tap, 0)

    def add_halos(a, carry):
        @pl.when(r > 0)
        def _():
            halo_down(a).wait_recv()

        @pl.when(r < STRIPS - 1)
        def _():
            halo_up(a).wait_recv()

        def edge(e, c):
            @pl.when(((e == 0) & (r > 0)) | ((e == 1) & (r < STRIPS - 1)))
            def _():
                add_row(a, e * (rows + 1))
            return c

        lax.fori_loop(0, 2, edge, 0)
        return carry

    load_k.wait()

    def own_row(i, carry):
        add_row(0, i + 1)
        return carry

    lax.fori_loop(0, rows, own_row, 0)

    def wave(q, carry):
        row = 1 + lax.rem(3 * q, 4)

        @pl.when(q == 3)
        def _():
            lax.fori_loop(0, slots, add_halos, 0)

        for h in range(2):
            @pl.when((f == 0) | (f == 2))
            def _(h=h):
                await_piece(2 - f // 2, q, h)
                relay_copy(q, h).start()

        for h in range(2):
            @pl.when(f < 2)
            def _(h=h):
                await_piece(1, q, h)

            @pl.when(f == 1)
            def _(h=h):
                await_piece(2, q, h)

        def send_halo(a, c):
            @pl.when((q == 0) & (r > 0))
            def _():
                halo_up(a).start()

            @pl.when((q == 1) & (r < STRIPS - 1))
            def _():
                halo_down(a).start()
            return c

        def slot_row(a, c):
            add_row(a, row)
            return c

        lax.fori_loop(1, slots, send_halo, 0)
        lax.fori_loop(1, slots, slot_row, 0)

        @pl.when(q == 0)
        def _():
            cur[1] = end_stage(0, near.at[0])
            send_stage(1, line_peers(f, r), far.at[0])

        @pl.when(q == 1)
        def _():
            total = over_group(end_stage(1, far.at[0]), channels) / cells_per
            centre = total[0:1]
            variance = jnp.maximum(total[1:2] - centre * centre, 0.0)
            stat_ref[0:1] = centre
            stat_ref[1:2] = lax.rsqrt(variance + EPS)

        @pl.when(q == 2)
        def _():
            def slope_row(y, c):
                normed = (xin[y].astype(jnp.float32) - stat_ref[0:1]) * stat_ref[1:2]
                preact = normed * gain_ref[...] + bias_ref[...]
                logistic = jax.nn.sigmoid(preact)
                slope[y] = logistic * (1.0 + preact * (1.0 - logistic)) * gain_ref[...]
                return c

            lax.fori_loop(0, rows, slope_row, 0)

        return carry

    lax.fori_loop(0, 4, wave, 0)

    def grad_row(y, carry):
        act_grad = (
            acc[y, pl.ds(PAD + 1, width), 0:channels]
            + acc[y, pl.ds(PAD, width), channels : 2 * channels]
            + acc[y, pl.ds(PAD - 1, width), 2 * channels : 3 * channels]
        )
        norm_grad = act_grad * slope[y]
        g_ref[y] = norm_grad
        normed = (xin[y].astype(jnp.float32) - stat_ref[0:1]) * stat_ref[1:2]
        return (
            carry[0] + jnp.sum(norm_grad, axis=0, keepdims=True),
            carry[1] + jnp.sum(norm_grad * normed, axis=0, keepdims=True),
        )

    first, second = lax.fori_loop(0, rows, grad_row, (zero, zero))
    cur[2] = jnp.concatenate([first, second], axis=0)
    send_stage(2, plane_peers(f, r), near.at[1])
    cur[3] = end_stage(2, near.at[1])
    send_stage(3, line_peers(f, r), far.at[1])

    @pl.when(f > 0)
    def _():
        for q in range(4):
            for h in range(2):
                own_copy(q, h).wait_send()

    @pl.when((f == 0) | (f == 2))
    def _():
        for q in range(4):
            for h in range(2):
                relay_copy(q, h).wait_send()

    def halo_sent(a, c):
        @pl.when(r > 0)
        def _():
            halo_up(a).wait_send()

        @pl.when(r < STRIPS - 1)
        def _():
            halo_down(a).wait_send()
        return c

    lax.fori_loop(0, slots, halo_sent, 0)
    total = over_group(end_stage(3, far.at[1]), channels) / cells_per
    stat_ref[2:4] = total
    for k, slots_ref in enumerate((near.at[0], far.at[0], near.at[1], far.at[1])):
        whole_stage(k, slots_ref).wait_send()


def shards(inputs, cotangent, kernel, norm_gain, norm_bias):
    _, rows, width, channels = inputs.shape
    cells_per = FRAMES * STRIPS * rows * width * (channels // GROUPS)
    vmem, anywhere = pl.BlockSpec(memory_space=pltpu.VMEM), pl.BlockSpec(memory_space=pl.ANY)
    dma = pltpu.SemaphoreType.DMA
    norm_grad, stats = pl.pallas_call(
        functools.partial(body, cells_per),
        out_shape=(
            jax.ShapeDtypeStruct((rows, width, channels), jnp.float32),
            jax.ShapeDtypeStruct((4, channels), jnp.float32),
        ),
        in_specs=[anywhere, anywhere, anywhere, vmem, vmem],
        out_specs=(vmem, vmem),
        scratch_shapes=[
            pltpu.VMEM((rows, width, channels), jnp.bfloat16),
            pltpu.VMEM((3, rows + 2, width, channels), jnp.bfloat16),
            pltpu.VMEM((3, 3, 3 * channels, channels), jnp.bfloat16),
            pltpu.VMEM((rows, width + 2 * PAD, 3 * channels), jnp.float32),
            pltpu.VMEM((rows, width, channels), jnp.float32),
            pltpu.VMEM((4, 2, channels), jnp.float32),
            pltpu.VMEM((2, 15, 2, channels), jnp.float32),
            pltpu.VMEM((2, 15, 2, channels), jnp.float32),
            dma((3,)), dma((4, 2)), dma((2, 4, 2)), dma((4, 2)),
            dma((3, 2)), dma((3, 2)), dma((4,)), dma((4,)),
        ],
        compiler_params=pltpu.CompilerParams(
            collective_id=0, has_side_effects=True, vmem_limit_bytes=48 << 20
        ),
    )(
        inputs, cotangent, kernel.reshape(3, 3, 3 * channels, channels),
        norm_gain[None], norm_bias[None],
    )
    normed = (inputs[0].astype(jnp.float32) - stats[0]) * stats[1]
    input_grad = stats[1] * (norm_grad - stats[2] - normed * stats[3])
    return input_grad.astype(jnp.bfloat16)[None]


def solution(mesh):
    placed = P("frames", "rows", None, None)
    return jax.shard_map(
        shards, mesh=mesh, in_specs=(placed, placed, P(), P(), P()), out_specs=placed, check_vma=False
    )
```

```python
import functools

import jax
import jax.numpy as jnp
from jax import lax
from jax.experimental import pallas as pl
from jax.experimental.pallas import tpu as pltpu
from jax.sharding import PartitionSpec as P

GROUPS = 32
EPS = 1e-06
MESH = pl.DeviceIdType.MESH
FRAMES, STRIPS = 4, 64
PAD = 8


def plane_peers(f, r):
    out = []
    for dy in range(4):
        for dx in range(4):
            if dy or dx:
                out.append((lax.rem(f + dy, 4), lax.rem(r + 16 * dx, 64)))
    return out


def line_peers(f, r):
    base, low = 16 * (r // 16), lax.rem(r, 16)
    return [(f, base + lax.rem(low + d, 16)) for d in range(1, 16)]


def over_group(total, channels):
    lane = lax.broadcasted_iota(jnp.int32, total.shape, 1)
    step = 1
    while step < channels // GROUPS:
        up = pltpu.roll(total, channels - step, 1)
        down = pltpu.roll(total, step, 1)
        total = total + jnp.where((lane // step) % 2 == 0, up, down)
        step *= 2
    return total


def body(
    cells_per, x_hbm, cot_hbm, k_hbm, gain_hbm, bias_hbm, g_ref, stat_ref,
    xin, gain_ref, bias_ref, staged, cot, weights, acc, slope, cur, near, far,
    lsem, ksem, own_send, frame_recv, relay_send, halo_send, halo_recv, ar_send, ar_recv,
):
    f, r = lax.axis_index("frames"), lax.axis_index("rows")
    rows, width, channels = xin.shape
    half = channels // 2
    slots = 3 - (f // 2) * (f - 1)

    def load_weights(k):
        return pltpu.make_async_copy(k_hbm.at[k], weights.at[k], ksem.at[k])

    load_cot = pltpu.make_async_copy(cot_hbm.at[0], staged, lsem.at[0])

    load_x = pltpu.make_async_copy(x_hbm.at[0], xin, lsem.at[2])
    load_gain = pltpu.make_async_copy(gain_hbm, gain_ref, lsem.at[3])
    load_bias = pltpu.make_async_copy(bias_hbm, bias_ref, lsem.at[4])
    load_x.start()
    load_cot.start()
    for k in (2, 1, 0):
        load_weights(k).start()
    load_gain.start()
    load_bias.start()

    barrier = pltpu.get_barrier_semaphore()
    greeted = plane_peers(f, r) + line_peers(f, r)
    greeted += [(f, lax.rem(r + 1, STRIPS)), (f, lax.rem(r + STRIPS - 1, STRIPS))]
    for peer in greeted:
        pl.semaphore_signal(barrier, inc=1, device_id=peer, device_id_type=MESH)

    load_x.wait()

    def add_stats(y, carry):
        values = xin[y].astype(jnp.float32)
        return (
            carry[0] + jnp.sum(values, axis=0, keepdims=True),
            carry[1] + jnp.sum(values * values, axis=0, keepdims=True),
        )

    zero = jnp.zeros((1, channels), jnp.float32)
    first, second = lax.fori_loop(0, rows, add_stats, (zero, zero))
    cur[0] = jnp.concatenate([first, second], axis=0)

    def contract(left, right):
        return lax.dot_general(
            left, right, (((1,), (1,)), ((), ())), preferred_element_type=jnp.float32
        )

    def row_of(p):
        return 1 + lax.rem(3 * (p // 2), 4)

    def piece(slot, p):
        return cot.at[slot, row_of(p), lax.rem(p, 2)]

    def own_copy(p):
        slot = 2 - lax.rem(f, 2)
        return pltpu.make_async_remote_copy(
            cot_hbm.at[0, row_of(p) - 1, :, pl.ds(pl.multiple_of(lax.rem(p, 2) * half, half), half)],
            piece(slot, p), own_send.at[p], frame_recv.at[slot - 1, p],
            device_id=((f // 3) * 2, r), device_id_type=MESH,
        )

    def relay_copy(p):
        source, slot = 2 - f // 2, 1 + f // 2
        return pltpu.make_async_remote_copy(
            piece(source, p), piece(slot, p), relay_send.at[p], frame_recv.at[slot - 1, p],
            device_id=(1, r), device_id_type=MESH,
        )

    def await_piece(slot, p):
        pltpu.make_async_remote_copy(
            piece(slot, p), piece(slot, p), own_send.at[p], frame_recv.at[slot - 1, p],
            device_id=(f, r), device_id_type=MESH,
        ).wait_recv()

    def halo_up(a):
        return pltpu.make_async_remote_copy(
            cot.at[a, 1], cot.at[a, rows + 1], halo_send.at[a, 0], halo_recv.at[a, 0],
            device_id=(f, lax.rem(r + STRIPS - 1, STRIPS)), device_id_type=MESH,
        )

    def halo_down(a):
        return pltpu.make_async_remote_copy(
            cot.at[a, rows], cot.at[a, 0], halo_send.at[a, 1], halo_recv.at[a, 1],
            device_id=(f, lax.rem(r + 1, STRIPS)), device_id_type=MESH,
        )

    def send_stage(k, peers, slots_ref):
        for j, peer in enumerate(peers):
            pltpu.make_async_remote_copy(
                cur.at[k], slots_ref.at[j], ar_send.at[k], ar_recv.at[k],
                device_id=peer, device_id_type=MESH,
            ).start()

    def whole_stage(k, slots_ref):
        return pltpu.make_async_remote_copy(
            slots_ref, slots_ref, ar_send.at[k], ar_recv.at[k],
            device_id=(f, r), device_id_type=MESH,
        )

    def end_stage(k, slots_ref):
        whole_stage(k, slots_ref).wait_recv()
        return cur[k] + jnp.sum(slots_ref[...], axis=0)

    def both_frames(i, h):
        lanes = pl.ds(pl.multiple_of(h * half, half), half)
        return jnp.concatenate([weights[1, i, :, lanes], weights[0, i, :, lanes]], axis=-1)

    def add_piece(row, h):
        def tap(b, carry):
            y = row - b

            @pl.when((y >= 0) & (y < rows))
            def _():
                acc[y, pl.ds(PAD, width), :] += contract(
                    jnp.concatenate([cot[1, row, h], cot[2, row, h]], axis=-1),
                    both_frames(2 - b, h),
                )
            return carry

        lax.fori_loop(0, 3, tap, 0)

    def await_halo(a, e):
        @pl.when((e == 0) & (r > 0))
        def _():
            halo_down(a).wait_recv()

        @pl.when((e == 1) & (r < STRIPS - 1))
        def _():
            halo_up(a).wait_recv()

    blank = jnp.zeros((2, width, half), jnp.bfloat16)

    @pl.when(r == 0)
    def _():
        for a in range(3):
            cot[a, 0] = blank

    @pl.when(r == STRIPS - 1)
    def _():
        for a in range(3):
            cot[a, rows + 1] = blank

    @pl.when(f == 2)
    def _():
        def clear(row, carry):
            cot[2, row] = blank
            return carry

        lax.fori_loop(0, rows + 2, clear, 0)

    load_cot.wait()

    def split_row(y, carry):
        for h in range(2):
            cot[0, y + 1, h] = staged[y, :, h * half : (h + 1) * half]
        return carry

    lax.fori_loop(0, rows, split_row, 0)
    pl.semaphore_wait(barrier, len(greeted))
    send_stage(0, plane_peers(f, r), near.at[0])

    def send_own(p, carry):
        own_copy(p).start()
        return carry

    ahead = 8 - 4 * lax.rem(f + 1, 2)

    @pl.when(f > 0)
    def _():
        lax.fori_loop(0, ahead, send_own, 0)

    @pl.when(r > 0)
    def _():
        halo_up(0).start()

    @pl.when(r < STRIPS - 1)
    def _():
        halo_down(0).start()

    edge_rows = jnp.zeros((rows, PAD, 3 * channels), jnp.float32)
    acc[:, 0:PAD, :] = edge_rows
    acc[:, PAD + width :, :] = edge_rows
    load_weights(2).wait()
    for b in (1, 0, 2):
        low, high = max(b, 1), min(b + rows, rows + 1)
        block = staged[low - 1 : high - 1]
        product = contract(
            block.reshape((high - low) * width, channels), weights[2, 2 - b]
        ).reshape(high - low, width, 3 * channels)
        if b == 1:
            acc[:, pl.ds(PAD, width), :] = product
        else:
            acc[low - b : high - b, pl.ds(PAD, width), :] += product

    for k in (1, 0):
        load_weights(k).wait()
    load_gain.wait()
    load_bias.wait()

    def wave(p, carry):
        row, h = row_of(p), lax.rem(p, 2)

        @pl.when(f > 0)
        def _():
            @pl.when(p + ahead < 8)
            def _():
                own_copy(p).wait_send()
                own_copy(p + ahead).start()

        @pl.when((f == 0) | (f == 2))
        def _():
            await_piece(2 - f // 2, p)
            relay_copy(p).start()

        @pl.when(f < 2)
        def _():
            await_piece(1, p)

        @pl.when(f == 1)
        def _():
            await_piece(2, p)

        def send_halo(a, c):
            @pl.when((p == 1) & (r > 0))
            def _():
                halo_up(a).start()

            @pl.when((p == 3) & (r < STRIPS - 1))
            def _():
                halo_down(a).start()
            return c

        lax.fori_loop(1, slots, send_halo, 0)

        @pl.when(f < 3)
        def _():
            add_piece(row, h)

        @pl.when((p == 4) | (p == 6))
        def _():
            e = (p - 4) // 2

            def wait_slot(a, c):
                await_halo(a, e)
                return c

            lax.fori_loop(1, slots, wait_slot, 0)

            @pl.when(f < 3)
            def _():
                def halo_half(h2, c):
                    y = e * (rows - 1)
                    acc[y, pl.ds(PAD, width), :] += contract(
                        jnp.concatenate([cot[1, y + 2 * e, h2], cot[2, y + 2 * e, h2]], axis=-1),
                        both_frames(2 - 2 * e, h2),
                    )
                    return c

                lax.fori_loop(0, 2, halo_half, 0)

        @pl.when(p == 1)
        def _():
            cur[1] = end_stage(0, near.at[0])
            send_stage(1, line_peers(f, r), far.at[0])

        @pl.when(p == 3)
        def _():
            def own_halo(e, c):
                await_halo(0, e)
                y = e * (rows - 1)
                acc[y, pl.ds(PAD, width), :] += contract(
                    jnp.concatenate([cot[0, y + 2 * e, 0], cot[0, y + 2 * e, 1]], axis=-1),
                    weights[2, 2 - 2 * e],
                )
                return c

            lax.fori_loop(0, 2, own_halo, 0)

        @pl.when(p == 4)
        def _():
            total = over_group(end_stage(1, far.at[0]), channels) / cells_per
            centre = total[0:1]
            variance = jnp.maximum(total[1:2] - centre * centre, 0.0)
            stat_ref[0:1] = centre
            stat_ref[1:2] = lax.rsqrt(variance + EPS)

            def slope_row(y, c):
                normed = (xin[y].astype(jnp.float32) - stat_ref[0:1]) * stat_ref[1:2]
                preact = normed * gain_ref[...] + bias_ref[...]
                logistic = jax.nn.sigmoid(preact)
                slope[y] = logistic * (1.0 + preact * (1.0 - logistic)) * gain_ref[...]
                return c

            lax.fori_loop(0, rows, slope_row, 0)

        return carry

    lax.fori_loop(0, 8, wave, 0)

    def grad_row(y, carry):
        act_grad = (
            acc[y, pl.ds(PAD + 1, width), 0:channels]
            + acc[y, pl.ds(PAD, width), channels : 2 * channels]
            + acc[y, pl.ds(PAD - 1, width), 2 * channels : 3 * channels]
        )
        norm_grad = act_grad * slope[y]
        g_ref[y] = norm_grad
        normed = (xin[y].astype(jnp.float32) - stat_ref[0:1]) * stat_ref[1:2]
        return (
            carry[0] + jnp.sum(norm_grad, axis=0, keepdims=True),
            carry[1] + jnp.sum(norm_grad * normed, axis=0, keepdims=True),
        )

    first, second = lax.fori_loop(0, rows, grad_row, (zero, zero))
    cur[2] = jnp.concatenate([first, second], axis=0)
    send_stage(2, plane_peers(f, r), near.at[1])
    cur[3] = end_stage(2, near.at[1])
    send_stage(3, line_peers(f, r), far.at[1])

    @pl.when(f > 0)
    def _():
        def own_sent(p, c):
            own_copy(p).wait_send()
            return c

        lax.fori_loop(8 - ahead, 8, own_sent, 0)

    @pl.when((f == 0) | (f == 2))
    def _():
        def sent(p, c):
            relay_copy(p).wait_send()
            return c

        lax.fori_loop(0, 8, sent, 0)

    def halo_sent(a, c):
        @pl.when(r > 0)
        def _():
            halo_up(a).wait_send()

        @pl.when(r < STRIPS - 1)
        def _():
            halo_down(a).wait_send()
        return c

    lax.fori_loop(0, slots, halo_sent, 0)
    total = over_group(end_stage(3, far.at[1]), channels) / cells_per
    stat_ref[2:4] = total
    for k, slots_ref in enumerate((near.at[0], far.at[0], near.at[1], far.at[1])):
        whole_stage(k, slots_ref).wait_send()


def shards(inputs, cotangent, kernel, norm_gain, norm_bias):
    _, rows, width, channels = inputs.shape
    cells_per = FRAMES * STRIPS * rows * width * (channels // GROUPS)
    vmem, anywhere = pl.BlockSpec(memory_space=pltpu.VMEM), pl.BlockSpec(memory_space=pltpu.HBM)
    dma = pltpu.SemaphoreType.DMA
    norm_grad, stats = pl.pallas_call(
        functools.partial(body, cells_per),
        out_shape=(
            jax.ShapeDtypeStruct((rows, width, channels), jnp.float32),
            jax.ShapeDtypeStruct((4, channels), jnp.float32),
        ),
        in_specs=[anywhere] * 5,
        out_specs=(vmem, vmem),
        scratch_shapes=[
            pltpu.VMEM((rows, width, channels), jnp.bfloat16),
            pltpu.VMEM((1, channels), jnp.float32),
            pltpu.VMEM((1, channels), jnp.float32),
            pltpu.VMEM((rows, width, channels), jnp.bfloat16),
            pltpu.VMEM((3, rows + 2, 2, width, channels // 2), jnp.bfloat16),
            pltpu.VMEM((3, 3, 3 * channels, channels), jnp.bfloat16),
            pltpu.VMEM((rows, width + 2 * PAD, 3 * channels), jnp.float32),
            pltpu.VMEM((rows, width, channels), jnp.float32),
            pltpu.VMEM((4, 2, channels), jnp.float32),
            pltpu.VMEM((2, 15, 2, channels), jnp.float32),
            pltpu.VMEM((2, 15, 2, channels), jnp.float32),
            dma((5,)), dma((3,)), dma((8,)), dma((2, 8)), dma((8,)),
            dma((3, 2)), dma((3, 2)), dma((4,)), dma((4,)),
        ],
        compiler_params=pltpu.CompilerParams(
            collective_id=0, has_side_effects=True, vmem_limit_bytes=61 << 20
        ),
    )(
        inputs, cotangent, kernel.reshape(3, 3, 3 * channels, channels),
        norm_gain[None], norm_bias[None],
    )
    normed = (inputs[0].astype(jnp.float32) - stats[0]) * stats[1]
    input_grad = stats[1] * (norm_grad - stats[2] - normed * stats[3])
    return input_grad.astype(jnp.bfloat16)[None]


def solution(mesh):
    placed = P("frames", "rows", None, None)
    return jax.shard_map(
        shards, mesh=mesh, in_specs=(placed, placed, P(), P(), P()), out_specs=placed, check_vma=False
    )
```

```python
import functools

import jax
import jax.numpy as jnp
from jax import lax
from jax.experimental import pallas as pl
from jax.experimental.pallas import tpu as pltpu
from jax.sharding import PartitionSpec as P

GROUPS = 32
EPS = 1e-06
MESH = pl.DeviceIdType.MESH
FRAMES, STRIPS = 4, 64
PAD = 8


def plane_peers(f, r):
    out = []
    for dy in range(4):
        for dx in range(4):
            if dy or dx:
                out.append((lax.rem(f + dy, 4), lax.rem(r + 16 * dx, 64)))
    return out


def line_peers(f, r):
    base, low = 16 * (r // 16), lax.rem(r, 16)
    return [(f, base + lax.rem(low + d, 16)) for d in range(1, 16)]


def over_group(total, channels):
    lane = lax.broadcasted_iota(jnp.int32, total.shape, 1)
    step = 1
    while step < channels // GROUPS:
        up = pltpu.roll(total, channels - step, 1)
        down = pltpu.roll(total, step, 1)
        total = total + jnp.where((lane // step) % 2 == 0, up, down)
        step *= 2
    return total


def body(
    cells_per, x_hbm, cot_hbm, k_hbm, gain_hbm, bias_hbm, out_ref,
    stat_ref, xin, gain_ref, bias_ref, staged, cot, weights, acc, slope, cur, near, far,
    lsem, ksem, own_send, frame_recv, relay_send, halo_send, halo_recv, ar_send, ar_recv,
):
    f, r = lax.axis_index("frames"), lax.axis_index("rows")
    rows, width, channels = xin.shape
    half = channels // 2
    slots = 3 - (f // 2) * (f - 1)

    def load_weights(k):
        return pltpu.make_async_copy(k_hbm.at[k], weights.at[k], ksem.at[k])

    load_cot = pltpu.make_async_copy(cot_hbm.at[0], staged, lsem.at[0])

    load_x = pltpu.make_async_copy(x_hbm.at[0], xin, lsem.at[2])
    load_gain = pltpu.make_async_copy(gain_hbm, gain_ref, lsem.at[3])
    load_bias = pltpu.make_async_copy(bias_hbm, bias_ref, lsem.at[4])
    load_x.start()
    load_cot.start()
    for k in (2, 1, 0):
        load_weights(k).start()
    load_gain.start()
    load_bias.start()

    barrier = pltpu.get_barrier_semaphore()
    greeted = plane_peers(f, r) + line_peers(f, r)
    greeted += [(f, lax.rem(r + 1, STRIPS)), (f, lax.rem(r + STRIPS - 1, STRIPS))]
    for peer in greeted:
        pl.semaphore_signal(barrier, inc=1, device_id=peer, device_id_type=MESH)

    load_x.wait()

    def add_stats(y, carry):
        values = xin[y].astype(jnp.float32)
        return (
            carry[0] + jnp.sum(values, axis=0, keepdims=True),
            carry[1] + jnp.sum(values * values, axis=0, keepdims=True),
        )

    zero = jnp.zeros((1, channels), jnp.float32)
    first, second = lax.fori_loop(0, rows, add_stats, (zero, zero))
    cur[0] = jnp.concatenate([first, second], axis=0)

    def contract(left, right):
        return lax.dot_general(
            left, right, (((1,), (1,)), ((), ())), preferred_element_type=jnp.float32
        )

    def row_of(p):
        return 1 + lax.rem(3 * (p // 2), 4)

    def piece(slot, p):
        return cot.at[slot, row_of(p), lax.rem(p, 2)]

    def own_copy(p):
        slot = 2 - lax.rem(f, 2)
        return pltpu.make_async_remote_copy(
            piece(0, p), piece(slot, p), own_send.at[p], frame_recv.at[slot - 1, p],
            device_id=((f // 3) * 2, r), device_id_type=MESH,
        )

    def relay_copy(p):
        source, slot = 2 - f // 2, 1 + f // 2
        return pltpu.make_async_remote_copy(
            piece(source, p), piece(slot, p), relay_send.at[p], frame_recv.at[slot - 1, p],
            device_id=(1, r), device_id_type=MESH,
        )

    def await_piece(slot, p):
        pltpu.make_async_remote_copy(
            piece(slot, p), piece(slot, p), own_send.at[p], frame_recv.at[slot - 1, p],
            device_id=(f, r), device_id_type=MESH,
        ).wait_recv()

    def halo_up(a):
        return pltpu.make_async_remote_copy(
            cot.at[a, 1], cot.at[a, rows + 1], halo_send.at[a, 0], halo_recv.at[a, 0],
            device_id=(f, lax.rem(r + STRIPS - 1, STRIPS)), device_id_type=MESH,
        )

    def halo_down(a):
        return pltpu.make_async_remote_copy(
            cot.at[a, rows], cot.at[a, 0], halo_send.at[a, 1], halo_recv.at[a, 1],
            device_id=(f, lax.rem(r + 1, STRIPS)), device_id_type=MESH,
        )

    def send_stage(k, peers, slots_ref):
        for j, peer in enumerate(peers):
            pltpu.make_async_remote_copy(
                cur.at[k], slots_ref.at[j], ar_send.at[k], ar_recv.at[k],
                device_id=peer, device_id_type=MESH,
            ).start()

    def whole_stage(k, slots_ref):
        return pltpu.make_async_remote_copy(
            slots_ref, slots_ref, ar_send.at[k], ar_recv.at[k],
            device_id=(f, r), device_id_type=MESH,
        )

    def end_stage(k, slots_ref):
        whole_stage(k, slots_ref).wait_recv()
        return cur[k] + jnp.sum(slots_ref[...], axis=0)

    def both_frames(i, h):
        lanes = pl.ds(pl.multiple_of(h * half, half), half)
        return jnp.concatenate([weights[1, i, :, lanes], weights[0, i, :, lanes]], axis=-1)

    def add_piece(row, h):
        def tap(b, carry):
            y = row - b

            @pl.when((y >= 0) & (y < rows))
            def _():
                acc[y, pl.ds(PAD, width), :] += contract(
                    jnp.concatenate([cot[1, row, h], cot[2, row, h]], axis=-1),
                    both_frames(2 - b, h),
                )
            return carry

        lax.fori_loop(0, 3, tap, 0)

    def await_halo(a, e):
        @pl.when((e == 0) & (r > 0))
        def _():
            halo_down(a).wait_recv()

        @pl.when((e == 1) & (r < STRIPS - 1))
        def _():
            halo_up(a).wait_recv()

    blank = jnp.zeros((2, width, half), jnp.bfloat16)

    @pl.when(r == 0)
    def _():
        for a in range(3):
            cot[a, 0] = blank

    @pl.when(r == STRIPS - 1)
    def _():
        for a in range(3):
            cot[a, rows + 1] = blank

    @pl.when(f == 2)
    def _():
        def clear(row, carry):
            cot[2, row] = blank
            return carry

        lax.fori_loop(0, rows + 2, clear, 0)

    load_cot.wait()

    def split_row(y, carry):
        for h in range(2):
            cot[0, y + 1, h] = staged[y, :, h * half : (h + 1) * half]
        return carry

    lax.fori_loop(0, rows, split_row, 0)
    pl.semaphore_wait(barrier, len(greeted))
    send_stage(0, plane_peers(f, r), near.at[0])

    def send_own(p, carry):
        own_copy(p).start()
        return carry

    ahead = 8 - 4 * lax.rem(f + 1, 2)

    @pl.when(f > 0)
    def _():
        lax.fori_loop(0, ahead, send_own, 0)

    @pl.when(r > 0)
    def _():
        halo_up(0).start()

    @pl.when(r < STRIPS - 1)
    def _():
        halo_down(0).start()

    edge_rows = jnp.zeros((rows, PAD, 3 * channels), jnp.float32)
    acc[:, 0:PAD, :] = edge_rows
    acc[:, PAD + width :, :] = edge_rows
    load_weights(2).wait()
    for b in (1, 0, 2):
        low, high = max(b, 1), min(b + rows, rows + 1)
        block = staged[low - 1 : high - 1]
        product = contract(
            block.reshape((high - low) * width, channels), weights[2, 2 - b]
        ).reshape(high - low, width, 3 * channels)
        if b == 1:
            acc[:, pl.ds(PAD, width), :] = product
        else:
            acc[low - b : high - b, pl.ds(PAD, width), :] += product

    for k in (1, 0):
        load_weights(k).wait()
    load_gain.wait()
    load_bias.wait()

    def wave(p, carry):
        row, h = row_of(p), lax.rem(p, 2)

        @pl.when(f > 0)
        def _():
            @pl.when(p + ahead < 8)
            def _():
                own_copy(p).wait_send()
                own_copy(p + ahead).start()

        @pl.when((f == 0) | (f == 2))
        def _():
            await_piece(2 - f // 2, p)
            relay_copy(p).start()

        @pl.when(f < 2)
        def _():
            await_piece(1, p)

        @pl.when(f == 1)
        def _():
            await_piece(2, p)

        def send_halo(a, c):
            @pl.when((p == 1) & (r > 0))
            def _():
                halo_up(a).start()

            @pl.when((p == 3) & (r < STRIPS - 1))
            def _():
                halo_down(a).start()
            return c

        lax.fori_loop(1, slots, send_halo, 0)

        @pl.when(f < 3)
        def _():
            add_piece(row, h)

        @pl.when((p == 5) | (p == 7))
        def _():
            e = (p - 5) // 2

            def wait_slot(a, c):
                await_halo(a, e)
                return c

            lax.fori_loop(1, slots, wait_slot, 0)

            @pl.when(f < 3)
            def _():
                def halo_half(h2, c):
                    y = e * (rows - 1)
                    acc[y, pl.ds(PAD, width), :] += contract(
                        jnp.concatenate([cot[1, y + 2 * e, h2], cot[2, y + 2 * e, h2]], axis=-1),
                        both_frames(2 - 2 * e, h2),
                    )
                    return c

                lax.fori_loop(0, 2, halo_half, 0)

        @pl.when(p == 0)
        def _():
            cur[1] = end_stage(0, near.at[0])
            send_stage(1, line_peers(f, r), far.at[0])

        @pl.when(p == 3)
        def _():
            def own_halo(e, c):
                await_halo(0, e)
                y = e * (rows - 1)
                acc[y, pl.ds(PAD, width), :] += contract(
                    jnp.concatenate([cot[0, y + 2 * e, 0], cot[0, y + 2 * e, 1]], axis=-1),
                    weights[2, 2 - 2 * e],
                )
                return c

            lax.fori_loop(0, 2, own_halo, 0)

        @pl.when(p == 3)
        def _():
            total = over_group(end_stage(1, far.at[0]), channels) / cells_per
            centre = total[0:1]
            variance = jnp.maximum(total[1:2] - centre * centre, 0.0)
            stat_ref[0:1] = centre
            stat_ref[1:2] = lax.rsqrt(variance + EPS)

            def slope_row(y, c):
                normed = (xin[y].astype(jnp.float32) - stat_ref[0:1]) * stat_ref[1:2]
                preact = normed * gain_ref[...] + bias_ref[...]
                logistic = jax.nn.sigmoid(preact)
                slope[y] = logistic * (1.0 + preact * (1.0 - logistic)) * gain_ref[...]
                return c

            lax.fori_loop(0, rows, slope_row, 0)

        return carry

    lax.fori_loop(0, 8, wave, 0)

    def grad_row(y, carry):
        act_grad = (
            acc[y, pl.ds(PAD + 1, width), 0:channels]
            + acc[y, pl.ds(PAD, width), channels : 2 * channels]
            + acc[y, pl.ds(PAD - 1, width), 2 * channels : 3 * channels]
        )
        norm_grad = act_grad * slope[y]
        slope[y] = norm_grad
        normed = (xin[y].astype(jnp.float32) - stat_ref[0:1]) * stat_ref[1:2]
        return (
            carry[0] + jnp.sum(norm_grad, axis=0, keepdims=True),
            carry[1] + jnp.sum(norm_grad * normed, axis=0, keepdims=True),
        )

    first, second = lax.fori_loop(0, rows, grad_row, (zero, zero))
    cur[2] = jnp.concatenate([first, second], axis=0)
    send_stage(2, plane_peers(f, r), near.at[1])
    cur[3] = end_stage(2, near.at[1])
    send_stage(3, line_peers(f, r), far.at[1])

    @pl.when(f > 0)
    def _():
        def own_sent(p, c):
            own_copy(p).wait_send()
            return c

        lax.fori_loop(8 - ahead, 8, own_sent, 0)

    @pl.when((f == 0) | (f == 2))
    def _():
        def sent(p, c):
            relay_copy(p).wait_send()
            return c

        lax.fori_loop(0, 8, sent, 0)

    def halo_sent(a, c):
        @pl.when(r > 0)
        def _():
            halo_up(a).wait_send()

        @pl.when(r < STRIPS - 1)
        def _():
            halo_down(a).wait_send()
        return c

    lax.fori_loop(0, slots, halo_sent, 0)
    total = over_group(end_stage(3, far.at[1]), channels) / cells_per
    stat_ref[2:4] = total

    def out_row(y, c):
        normed = (xin[y].astype(jnp.float32) - stat_ref[0:1]) * stat_ref[1:2]
        input_grad = stat_ref[1:2] * (slope[y] - stat_ref[2:3] - normed * stat_ref[3:4])
        out_ref[0, y] = input_grad.astype(jnp.bfloat16)
        return c

    lax.fori_loop(0, rows, out_row, 0)
    for k, slots_ref in enumerate((near.at[0], far.at[0], near.at[1], far.at[1])):
        whole_stage(k, slots_ref).wait_send()


def shards(inputs, cotangent, kernel, norm_gain, norm_bias):
    _, rows, width, channels = inputs.shape
    cells_per = FRAMES * STRIPS * rows * width * (channels // GROUPS)
    vmem, anywhere = pl.BlockSpec(memory_space=pltpu.VMEM), pl.BlockSpec(memory_space=pltpu.HBM)
    dma = pltpu.SemaphoreType.DMA
    return pl.pallas_call(
        functools.partial(body, cells_per),
        out_shape=jax.ShapeDtypeStruct(inputs.shape, jnp.bfloat16),
        in_specs=[anywhere] * 5,
        out_specs=vmem,
        scratch_shapes=[
            pltpu.VMEM((4, channels), jnp.float32),
            pltpu.VMEM((rows, width, channels), jnp.bfloat16),
            pltpu.VMEM((1, channels), jnp.float32),
            pltpu.VMEM((1, channels), jnp.float32),
            pltpu.VMEM((rows, width, channels), jnp.bfloat16),
            pltpu.VMEM((3, rows + 2, 2, width, channels // 2), jnp.bfloat16),
            pltpu.VMEM((3, 3, 3 * channels, channels), jnp.bfloat16),
            pltpu.VMEM((rows, width + 2 * PAD, 3 * channels), jnp.float32),
            pltpu.VMEM((rows, width, channels), jnp.float32),
            pltpu.VMEM((4, 2, channels), jnp.float32),
            pltpu.VMEM((2, 15, 2, channels), jnp.float32),
            pltpu.VMEM((2, 15, 2, channels), jnp.float32),
            dma((5,)), dma((3,)), dma((8,)), dma((2, 8)), dma((8,)),
            dma((3, 2)), dma((3, 2)), dma((4,)), dma((4,)),
        ],
        compiler_params=pltpu.CompilerParams(
            collective_id=0, has_side_effects=True, vmem_limit_bytes=61 << 20
        ),
    )(
        inputs, cotangent, kernel.reshape(3, 3, 3 * channels, channels),
        norm_gain[None], norm_bias[None],
    )


def solution(mesh):
    placed = P("frames", "rows", None, None)
    return jax.shard_map(
        shards, mesh=mesh, in_specs=(placed, placed, P(), P(), P()), out_specs=placed, check_vma=False
    )
```

```python
import functools

import jax
import jax.numpy as jnp
from jax import lax
from jax.experimental import pallas as pl
from jax.experimental.pallas import tpu as pltpu
from jax.sharding import PartitionSpec as P

GROUPS = 32
EPS = 1e-06
MESH = pl.DeviceIdType.MESH
FRAMES, STRIPS = 4, 64
PAD = 8
FIRST = 1
FAR_FIRST = (8, 7, 9, 6, 10, 5, 11, 4, 12, 3, 13, 2, 14, 1, 15)


def plane_peers(f, r):
    offsets = [(dy, dx) for dy in (2, 1, 3, 0) for dx in (2, 1, 3, 0)]
    offsets.sort(key=lambda o: -sum(min(d, 4 - d) for d in o))
    return [(lax.rem(f + dy, 4), lax.rem(r + 16 * dx, 64)) for dy, dx in offsets[:-1]]


def line_peers(f, r):
    base, low = 16 * (r // 16), lax.rem(r, 16)
    return [(f, base + lax.rem(low + d, 16)) for d in FAR_FIRST]


def over_group(total, channels):
    lane = lax.broadcasted_iota(jnp.int32, total.shape, 1)
    step = 1
    while step < channels // GROUPS:
        up = pltpu.roll(total, channels - step, 1)
        down = pltpu.roll(total, step, 1)
        total = total + jnp.where((lane // step) % 2 == 0, up, down)
        step *= 2
    return total


def body(
    cells_per, x_hbm, cot_hbm, k_hbm, gain_hbm, bias_hbm, out_ref,
    stat_ref, xin, gain_ref, bias_ref, staged, cot, weights, acc, slope, cur, near, far,
    lsem, ksem, own_send, frame_recv, relay_send, halo_send, halo_recv, ar_send, ar_recv,
):
    f, r = lax.axis_index("frames"), lax.axis_index("rows")
    rows, width, channels = xin.shape
    half = channels // 2
    slots = 3 - (f // 2) * (f - 1)

    def load_weights(k):
        return pltpu.make_async_copy(k_hbm.at[k], weights.at[k], ksem.at[k])

    load_cot = pltpu.make_async_copy(cot_hbm.at[0], staged, lsem.at[0])

    load_x = pltpu.make_async_copy(x_hbm.at[0], xin, lsem.at[2])
    load_gain = pltpu.make_async_copy(gain_hbm, gain_ref, lsem.at[3])
    load_bias = pltpu.make_async_copy(bias_hbm, bias_ref, lsem.at[4])
    load_x.start()
    load_cot.start()
    for k in (2, 1, 0):
        load_weights(k).start()
    load_gain.start()
    load_bias.start()

    barrier = pltpu.get_barrier_semaphore()
    greeted = plane_peers(f, r) + line_peers(f, r)
    greeted += [(f, lax.rem(r + 1, STRIPS)), (f, lax.rem(r + STRIPS - 1, STRIPS))]
    for peer in greeted:
        pl.semaphore_signal(barrier, inc=1, device_id=peer, device_id_type=MESH)

    def contract(left, right):
        return lax.dot_general(
            left, right, (((1,), (1,)), ((), ())), preferred_element_type=jnp.float32
        )

    def row_of(p):
        return 1 + lax.rem(3 * (p // 2), 4)

    def piece(slot, p):
        return cot.at[slot, row_of(p), lax.rem(p, 2)]

    def own_copy(p):
        slot = 2 - lax.rem(f, 2)
        return pltpu.make_async_remote_copy(
            piece(0, p), piece(slot, p), own_send.at[p], frame_recv.at[slot - 1, p],
            device_id=((f // 3) * 2, r), device_id_type=MESH,
        )

    def relay_copy(p):
        source, slot = 2 - f // 2, 1 + f // 2
        return pltpu.make_async_remote_copy(
            piece(source, p), piece(slot, p), relay_send.at[p], frame_recv.at[slot - 1, p],
            device_id=(1, r), device_id_type=MESH,
        )

    def await_piece(slot, p):
        pltpu.make_async_remote_copy(
            piece(slot, p), piece(slot, p), own_send.at[p], frame_recv.at[slot - 1, p],
            device_id=(f, r), device_id_type=MESH,
        ).wait_recv()

    def halo_up(a):
        return pltpu.make_async_remote_copy(
            cot.at[a, 1], cot.at[a, rows + 1], halo_send.at[a, 0], halo_recv.at[a, 0],
            device_id=(f, lax.rem(r + STRIPS - 1, STRIPS)), device_id_type=MESH,
        )

    def halo_down(a):
        return pltpu.make_async_remote_copy(
            cot.at[a, rows], cot.at[a, 0], halo_send.at[a, 1], halo_recv.at[a, 1],
            device_id=(f, lax.rem(r + 1, STRIPS)), device_id_type=MESH,
        )

    def send_stage(k, peers, slots_ref):
        for j, peer in enumerate(peers):
            pltpu.make_async_remote_copy(
                cur.at[k], slots_ref.at[j], ar_send.at[k], ar_recv.at[k],
                device_id=peer, device_id_type=MESH,
            ).start()

    def whole_stage(k, slots_ref):
        return pltpu.make_async_remote_copy(
            slots_ref, slots_ref, ar_send.at[k], ar_recv.at[k],
            device_id=(f, r), device_id_type=MESH,
        )

    def end_stage(k, slots_ref):
        whole_stage(k, slots_ref).wait_recv()
        return cur[k] + jnp.sum(slots_ref[...], axis=0)

    def both_frames(i, h):
        lanes = pl.ds(pl.multiple_of(h * half, half), half)
        return jnp.concatenate([weights[1, i, :, lanes], weights[0, i, :, lanes]], axis=-1)

    def add_piece(row, h):
        def tap(b, carry):
            y = row - b

            @pl.when((y >= 0) & (y < rows))
            def _():
                acc[y, pl.ds(PAD, width), :] += contract(
                    jnp.concatenate([cot[1, row, h], cot[2, row, h]], axis=-1),
                    both_frames(2 - b, h),
                )
            return carry

        lax.fori_loop(0, 3, tap, 0)

    def await_halo(a, e):
        @pl.when((e == 0) & (r > 0))
        def _():
            halo_down(a).wait_recv()

        @pl.when((e == 1) & (r < STRIPS - 1))
        def _():
            halo_up(a).wait_recv()

    blank = jnp.zeros((2, width, half), jnp.bfloat16)

    @pl.when(r == 0)
    def _():
        for a in range(3):
            cot[a, 0] = blank

    @pl.when(r == STRIPS - 1)
    def _():
        for a in range(3):
            cot[a, rows + 1] = blank

    @pl.when(f == 2)
    def _():
        def clear(row, carry):
            cot[2, row] = blank
            return carry

        lax.fori_loop(0, rows + 2, clear, 0)

    load_cot.wait()

    def split_row(y, carry):
        for h in range(2):
            cot[0, y + 1, h] = staged[y, :, h * half : (h + 1) * half]
        return carry

    lax.fori_loop(0, rows, split_row, 0)
    pl.semaphore_wait(barrier, len(greeted))

    def send_own(p, carry):
        own_copy(p).start()
        return carry

    ahead = 8 - 4 * lax.rem(f + 1, 2)

    @pl.when(f > 0)
    def _():
        lax.fori_loop(0, FIRST, send_own, 0)

    load_x.wait()

    def add_stats(y, carry):
        values = xin[y].astype(jnp.float32)
        return (
            carry[0] + jnp.sum(values, axis=0, keepdims=True),
            carry[1] + jnp.sum(values * values, axis=0, keepdims=True),
        )

    zero = jnp.zeros((1, channels), jnp.float32)
    first, second = lax.fori_loop(0, rows, add_stats, (zero, zero))
    cur[0] = jnp.concatenate([first, second], axis=0)

    send_stage(0, plane_peers(f, r), near.at[0])

    @pl.when(f > 0)
    def _():
        lax.fori_loop(FIRST, ahead, send_own, 0)

    @pl.when(r > 0)
    def _():
        halo_up(0).start()

    @pl.when(r < STRIPS - 1)
    def _():
        halo_down(0).start()

    edge_rows = jnp.zeros((rows, PAD, 3 * channels), jnp.float32)
    acc[:, 0:PAD, :] = edge_rows
    acc[:, PAD + width :, :] = edge_rows
    load_weights(2).wait()
    for b in (1, 0, 2):
        low, high = max(b, 1), min(b + rows, rows + 1)
        block = staged[low - 1 : high - 1]
        product = contract(
            block.reshape((high - low) * width, channels), weights[2, 2 - b]
        ).reshape(high - low, width, 3 * channels)
        if b == 1:
            acc[:, pl.ds(PAD, width), :] = product
        else:
            acc[low - b : high - b, pl.ds(PAD, width), :] += product

    for k in (1, 0):
        load_weights(k).wait()
    load_gain.wait()
    load_bias.wait()

    def wave(p, carry):
        row, h = row_of(p), lax.rem(p, 2)

        @pl.when(f > 0)
        def _():
            @pl.when(p + ahead < 8)
            def _():
                own_copy(p).wait_send()
                own_copy(p + ahead).start()

        @pl.when((f == 0) | (f == 2))
        def _():
            await_piece(2 - f // 2, p)
            relay_copy(p).start()

        @pl.when(f < 2)
        def _():
            await_piece(1, p)

        @pl.when(f == 1)
        def _():
            await_piece(2, p)

        def send_halo(a, c):
            @pl.when((p == 1) & (r > 0))
            def _():
                halo_up(a).start()

            @pl.when((p == 3) & (r < STRIPS - 1))
            def _():
                halo_down(a).start()
            return c

        lax.fori_loop(1, slots, send_halo, 0)

        @pl.when(f < 3)
        def _():
            add_piece(row, h)

        @pl.when((p == 5) | (p == 7))
        def _():
            e = (p - 5) // 2

            def wait_slot(a, c):
                await_halo(a, e)
                return c

            lax.fori_loop(1, slots, wait_slot, 0)

            @pl.when(f < 3)
            def _():
                def halo_half(h2, c):
                    y = e * (rows - 1)
                    acc[y, pl.ds(PAD, width), :] += contract(
                        jnp.concatenate([cot[1, y + 2 * e, h2], cot[2, y + 2 * e, h2]], axis=-1),
                        both_frames(2 - 2 * e, h2),
                    )
                    return c

                lax.fori_loop(0, 2, halo_half, 0)

        @pl.when(p == 0)
        def _():
            cur[1] = end_stage(0, near.at[0])
            send_stage(1, line_peers(f, r), far.at[0])

        @pl.when(p == 3)
        def _():
            def own_halo(e, c):
                await_halo(0, e)
                y = e * (rows - 1)
                acc[y, pl.ds(PAD, width), :] += contract(
                    jnp.concatenate([cot[0, y + 2 * e, 0], cot[0, y + 2 * e, 1]], axis=-1),
                    weights[2, 2 - 2 * e],
                )
                return c

            lax.fori_loop(0, 2, own_halo, 0)

        @pl.when(p == 3)
        def _():
            total = over_group(end_stage(1, far.at[0]), channels) / cells_per
            centre = total[0:1]
            variance = jnp.maximum(total[1:2] - centre * centre, 0.0)
            stat_ref[0:1] = centre
            stat_ref[1:2] = lax.rsqrt(variance + EPS)

            def slope_row(y, c):
                normed = (xin[y].astype(jnp.float32) - stat_ref[0:1]) * stat_ref[1:2]
                preact = normed * gain_ref[...] + bias_ref[...]
                logistic = jax.nn.sigmoid(preact)
                slope[y] = logistic * (1.0 + preact * (1.0 - logistic)) * gain_ref[...]
                return c

            lax.fori_loop(0, rows, slope_row, 0)

        return carry

    lax.fori_loop(0, 8, wave, 0)

    def grad_row(y, carry):
        act_grad = (
            acc[y, pl.ds(PAD + 1, width), 0:channels]
            + acc[y, pl.ds(PAD, width), channels : 2 * channels]
            + acc[y, pl.ds(PAD - 1, width), 2 * channels : 3 * channels]
        )
        norm_grad = act_grad * slope[y]
        slope[y] = norm_grad
        normed = (xin[y].astype(jnp.float32) - stat_ref[0:1]) * stat_ref[1:2]
        return (
            carry[0] + jnp.sum(norm_grad, axis=0, keepdims=True),
            carry[1] + jnp.sum(norm_grad * normed, axis=0, keepdims=True),
        )

    first, second = lax.fori_loop(0, rows, grad_row, (zero, zero))
    cur[2] = jnp.concatenate([first, second], axis=0)
    send_stage(2, plane_peers(f, r), near.at[1])
    cur[3] = end_stage(2, near.at[1])
    send_stage(3, line_peers(f, r), far.at[1])

    @pl.when(f > 0)
    def _():
        def own_sent(p, c):
            own_copy(p).wait_send()
            return c

        lax.fori_loop(8 - ahead, 8, own_sent, 0)

    @pl.when((f == 0) | (f == 2))
    def _():
        def sent(p, c):
            relay_copy(p).wait_send()
            return c

        lax.fori_loop(0, 8, sent, 0)

    def halo_sent(a, c):
        @pl.when(r > 0)
        def _():
            halo_up(a).wait_send()

        @pl.when(r < STRIPS - 1)
        def _():
            halo_down(a).wait_send()
        return c

    lax.fori_loop(0, slots, halo_sent, 0)
    total = over_group(end_stage(3, far.at[1]), channels) / cells_per
    stat_ref[2:4] = total

    def out_row(y, c):
        normed = (xin[y].astype(jnp.float32) - stat_ref[0:1]) * stat_ref[1:2]
        input_grad = stat_ref[1:2] * (slope[y] - stat_ref[2:3] - normed * stat_ref[3:4])
        out_ref[0, y] = input_grad.astype(jnp.bfloat16)
        return c

    lax.fori_loop(0, rows, out_row, 0)
    for k, slots_ref in enumerate((near.at[0], far.at[0], near.at[1], far.at[1])):
        whole_stage(k, slots_ref).wait_send()


def shards(inputs, cotangent, kernel, norm_gain, norm_bias):
    _, rows, width, channels = inputs.shape
    cells_per = FRAMES * STRIPS * rows * width * (channels // GROUPS)
    vmem, anywhere = pl.BlockSpec(memory_space=pltpu.VMEM), pl.BlockSpec(memory_space=pltpu.HBM)
    dma = pltpu.SemaphoreType.DMA
    return pl.pallas_call(
        functools.partial(body, cells_per),
        out_shape=jax.ShapeDtypeStruct(inputs.shape, jnp.bfloat16),
        in_specs=[anywhere] * 5,
        out_specs=vmem,
        scratch_shapes=[
            pltpu.VMEM((4, channels), jnp.float32),
            pltpu.VMEM((rows, width, channels), jnp.bfloat16),
            pltpu.VMEM((1, channels), jnp.float32),
            pltpu.VMEM((1, channels), jnp.float32),
            pltpu.VMEM((rows, width, channels), jnp.bfloat16),
            pltpu.VMEM((3, rows + 2, 2, width, channels // 2), jnp.bfloat16),
            pltpu.VMEM((3, 3, 3 * channels, channels), jnp.bfloat16),
            pltpu.VMEM((rows, width + 2 * PAD, 3 * channels), jnp.float32),
            pltpu.VMEM((rows, width, channels), jnp.float32),
            pltpu.VMEM((4, 2, channels), jnp.float32),
            pltpu.VMEM((2, 15, 2, channels), jnp.float32),
            pltpu.VMEM((2, 15, 2, channels), jnp.float32),
            dma((5,)), dma((3,)), dma((8,)), dma((2, 8)), dma((8,)),
            dma((3, 2)), dma((3, 2)), dma((4,)), dma((4,)),
        ],
        compiler_params=pltpu.CompilerParams(
            collective_id=0, has_side_effects=True, vmem_limit_bytes=61 << 20
        ),
    )(
        inputs, cotangent, kernel.reshape(3, 3, 3 * channels, channels),
        norm_gain[None], norm_bias[None],
    )


def solution(mesh):
    placed = P("frames", "rows", None, None)
    return jax.shard_map(
        shards, mesh=mesh, in_specs=(placed, placed, P(), P(), P()), out_specs=placed, check_vma=False
    )
```

```python
import functools

import jax
import jax.numpy as jnp
from jax import lax
from jax.experimental import pallas as pl
from jax.experimental.pallas import tpu as pltpu
from jax.sharding import PartitionSpec as P

GROUPS = 32
EPS = 1e-06
MESH = pl.DeviceIdType.MESH
FRAMES, STRIPS = 4, 64
PAD = 8
FIRST = 1
FAR_FIRST = (8, 7, 9, 6, 10, 5, 11, 4, 12, 3, 13, 2, 14, 1, 15)


def plane_peers(f, r):
    offsets = [(dy, dx) for dy in (2, 1, 3, 0) for dx in (2, 1, 3, 0)]
    offsets.sort(key=lambda o: -sum(min(d, 4 - d) for d in o))
    return [(lax.rem(f + dy, 4), lax.rem(r + 16 * dx, 64)) for dy, dx in offsets[:-1]]


def line_peers(f, r):
    base, low = 16 * (r // 16), lax.rem(r, 16)
    return [(f, base + lax.rem(low + d, 16)) for d in FAR_FIRST]


def over_group(total, channels):
    lane = lax.broadcasted_iota(jnp.int32, total.shape, 1)
    step = 1
    while step < channels // GROUPS:
        up = pltpu.roll(total, channels - step, 1)
        down = pltpu.roll(total, step, 1)
        total = total + jnp.where((lane // step) % 2 == 0, up, down)
        step *= 2
    return total


def body(
    cells_per, x_hbm, cot_hbm, k_hbm, gain_hbm, bias_hbm, out_ref,
    stat_ref, xin, gain_ref, bias_ref, staged, cot, weights, acc, slope, cur, near, far,
    lsem, ksem, own_send, frame_recv, relay_send, halo_send, halo_recv, ar_send, ar_recv,
):
    f, r = lax.axis_index("frames"), lax.axis_index("rows")
    rows, width, channels = xin.shape
    half = channels // 2
    slots = 3 - (f // 2) * (f - 1)

    def load_weights(k):
        return pltpu.make_async_copy(k_hbm.at[k], weights.at[k], ksem.at[k])

    load_cot = pltpu.make_async_copy(cot_hbm.at[0], staged, lsem.at[0])

    load_x = pltpu.make_async_copy(x_hbm.at[0], xin, lsem.at[2])
    load_gain = pltpu.make_async_copy(gain_hbm, gain_ref, lsem.at[3])
    load_bias = pltpu.make_async_copy(bias_hbm, bias_ref, lsem.at[4])
    load_cot.start()
    load_x.start()
    for k in (2, 1, 0):
        load_weights(k).start()
    load_gain.start()
    load_bias.start()

    barrier = pltpu.get_barrier_semaphore()
    greeted = plane_peers(f, r) + line_peers(f, r)
    greeted += [(f, lax.rem(r + 1, STRIPS)), (f, lax.rem(r + STRIPS - 1, STRIPS))]
    for peer in greeted:
        pl.semaphore_signal(barrier, inc=1, device_id=peer, device_id_type=MESH)

    def contract(left, right):
        return lax.dot_general(
            left, right, (((1,), (1,)), ((), ())), preferred_element_type=jnp.float32
        )

    def row_of(p):
        return 1 + lax.rem(3 * (p // 2), 4)

    def piece(slot, p):
        return cot.at[slot, row_of(p), lax.rem(p, 2)]

    def own_copy(p):
        slot = 2 - lax.rem(f, 2)
        return pltpu.make_async_remote_copy(
            piece(0, p), piece(slot, p), own_send.at[p], frame_recv.at[slot - 1, p],
            device_id=((f // 3) * 2, r), device_id_type=MESH,
        )

    def relay_copy(p):
        source, slot = 2 - f // 2, 1 + f // 2
        return pltpu.make_async_remote_copy(
            piece(source, p), piece(slot, p), relay_send.at[p], frame_recv.at[slot - 1, p],
            device_id=(1, r), device_id_type=MESH,
        )

    def await_piece(slot, p):
        pltpu.make_async_remote_copy(
            piece(slot, p), piece(slot, p), own_send.at[p], frame_recv.at[slot - 1, p],
            device_id=(f, r), device_id_type=MESH,
        ).wait_recv()

    def halo_up(a):
        return pltpu.make_async_remote_copy(
            cot.at[a, 1], cot.at[a, rows + 1], halo_send.at[a, 0], halo_recv.at[a, 0],
            device_id=(f, lax.rem(r + STRIPS - 1, STRIPS)), device_id_type=MESH,
        )

    def halo_down(a):
        return pltpu.make_async_remote_copy(
            cot.at[a, rows], cot.at[a, 0], halo_send.at[a, 1], halo_recv.at[a, 1],
            device_id=(f, lax.rem(r + 1, STRIPS)), device_id_type=MESH,
        )

    def send_stage(k, peers, slots_ref):
        for j, peer in enumerate(peers):
            pltpu.make_async_remote_copy(
                cur.at[k], slots_ref.at[j], ar_send.at[k], ar_recv.at[k],
                device_id=peer, device_id_type=MESH,
            ).start()

    def whole_stage(k, slots_ref):
        return pltpu.make_async_remote_copy(
            slots_ref, slots_ref, ar_send.at[k], ar_recv.at[k],
            device_id=(f, r), device_id_type=MESH,
        )

    def end_stage(k, slots_ref):
        whole_stage(k, slots_ref).wait_recv()
        return cur[k] + jnp.sum(slots_ref[...], axis=0)

    def both_frames(i, h):
        lanes = pl.ds(pl.multiple_of(h * half, half), half)
        return jnp.concatenate([weights[1, i, :, lanes], weights[0, i, :, lanes]], axis=-1)

    def add_piece(row, h):
        def tap(b, carry):
            y = row - b

            @pl.when((y >= 0) & (y < rows))
            def _():
                acc[y, pl.ds(PAD, width), :] += contract(
                    jnp.concatenate([cot[1, row, h], cot[2, row, h]], axis=-1),
                    both_frames(2 - b, h),
                )
            return carry

        lax.fori_loop(0, 3, tap, 0)

    def await_halo(a, e):
        @pl.when((e == 0) & (r > 0))
        def _():
            halo_down(a).wait_recv()

        @pl.when((e == 1) & (r < STRIPS - 1))
        def _():
            halo_up(a).wait_recv()

    blank = jnp.zeros((2, width, half), jnp.bfloat16)

    @pl.when(r == 0)
    def _():
        for a in range(3):
            cot[a, 0] = blank

    @pl.when(r == STRIPS - 1)
    def _():
        for a in range(3):
            cot[a, rows + 1] = blank

    @pl.when(f == 2)
    def _():
        def clear(row, carry):
            cot[2, row] = blank
            return carry

        lax.fori_loop(0, rows + 2, clear, 0)

    load_cot.wait()

    def split_row(y, carry):
        for h in range(2):
            cot[0, y + 1, h] = staged[y, :, h * half : (h + 1) * half]
        return carry

    lax.fori_loop(0, rows, split_row, 0)
    pl.semaphore_wait(barrier, len(greeted))

    def send_own(p, carry):
        own_copy(p).start()
        return carry

    ahead = 8 - 4 * lax.rem(f + 1, 2)

    @pl.when(f > 0)
    def _():
        lax.fori_loop(0, FIRST, send_own, 0)

    load_x.wait()

    def add_stats(y, carry):
        values = xin[y].astype(jnp.float32)
        return (
            carry[0] + jnp.sum(values, axis=0, keepdims=True),
            carry[1] + jnp.sum(values * values, axis=0, keepdims=True),
        )

    zero = jnp.zeros((1, channels), jnp.float32)
    first, second = lax.fori_loop(0, rows, add_stats, (zero, zero))
    cur[0] = jnp.concatenate([first, second], axis=0)

    send_stage(0, plane_peers(f, r), near.at[0])

    @pl.when(r > 0)
    def _():
        halo_up(0).start()

    @pl.when(r < STRIPS - 1)
    def _():
        halo_down(0).start()

    @pl.when(f > 0)
    def _():
        lax.fori_loop(FIRST, ahead, send_own, 0)

    edge_rows = jnp.zeros((rows, PAD, 3 * channels), jnp.float32)
    acc[:, 0:PAD, :] = edge_rows
    acc[:, PAD + width :, :] = edge_rows
    load_weights(2).wait()
    for b in (1, 0, 2):
        low, high = max(b, 1), min(b + rows, rows + 1)
        block = staged[low - 1 : high - 1]
        product = contract(
            block.reshape((high - low) * width, channels), weights[2, 2 - b]
        ).reshape(high - low, width, 3 * channels)
        if b == 1:
            acc[:, pl.ds(PAD, width), :] = product
        else:
            acc[low - b : high - b, pl.ds(PAD, width), :] += product

    for k in (1, 0):
        load_weights(k).wait()
    load_gain.wait()
    load_bias.wait()

    def wave(p, carry):
        row, h = row_of(p), lax.rem(p, 2)

        @pl.when(f > 0)
        def _():
            @pl.when(p + ahead < 8)
            def _():
                own_copy(p).wait_send()
                own_copy(p + ahead).start()

        @pl.when((f == 0) | (f == 2))
        def _():
            await_piece(2 - f // 2, p)
            relay_copy(p).start()

        @pl.when(f < 2)
        def _():
            await_piece(1, p)

        @pl.when(f == 1)
        def _():
            await_piece(2, p)

        def send_halo(a, c):
            @pl.when((p == 1) & (r > 0))
            def _():
                halo_up(a).start()

            @pl.when((p == 3) & (r < STRIPS - 1))
            def _():
                halo_down(a).start()
            return c

        lax.fori_loop(1, slots, send_halo, 0)

        @pl.when(f < 3)
        def _():
            add_piece(row, h)

        @pl.when((p == 5) | (p == 7))
        def _():
            e = (p - 5) // 2

            def wait_slot(a, c):
                await_halo(a, e)
                return c

            lax.fori_loop(1, slots, wait_slot, 0)

            @pl.when(f < 3)
            def _():
                def halo_half(h2, c):
                    y = e * (rows - 1)
                    acc[y, pl.ds(PAD, width), :] += contract(
                        jnp.concatenate([cot[1, y + 2 * e, h2], cot[2, y + 2 * e, h2]], axis=-1),
                        both_frames(2 - 2 * e, h2),
                    )
                    return c

                lax.fori_loop(0, 2, halo_half, 0)

        @pl.when(p == 0)
        def _():
            cur[1] = end_stage(0, near.at[0])
            send_stage(1, line_peers(f, r), far.at[0])

        @pl.when(p == 3)
        def _():
            def own_halo(e, c):
                await_halo(0, e)
                y = e * (rows - 1)
                acc[y, pl.ds(PAD, width), :] += contract(
                    jnp.concatenate([cot[0, y + 2 * e, 0], cot[0, y + 2 * e, 1]], axis=-1),
                    weights[2, 2 - 2 * e],
                )
                return c

            lax.fori_loop(0, 2, own_halo, 0)

        @pl.when(p == 3)
        def _():
            total = over_group(end_stage(1, far.at[0]), channels) / cells_per
            centre = total[0:1]
            variance = jnp.maximum(total[1:2] - centre * centre, 0.0)
            stat_ref[0:1] = centre
            stat_ref[1:2] = lax.rsqrt(variance + EPS)

            def slope_row(y, c):
                normed = (xin[y].astype(jnp.float32) - stat_ref[0:1]) * stat_ref[1:2]
                preact = normed * gain_ref[...] + bias_ref[...]
                logistic = jax.nn.sigmoid(preact)
                slope[y] = logistic * (1.0 + preact * (1.0 - logistic)) * gain_ref[...]
                return c

            lax.fori_loop(0, rows, slope_row, 0)

        return carry

    lax.fori_loop(0, 8, wave, 0)

    def grad_row(y, carry):
        act_grad = (
            acc[y, pl.ds(PAD + 1, width), 0:channels]
            + acc[y, pl.ds(PAD, width), channels : 2 * channels]
            + acc[y, pl.ds(PAD - 1, width), 2 * channels : 3 * channels]
        )
        norm_grad = act_grad * slope[y]
        slope[y] = norm_grad
        normed = (xin[y].astype(jnp.float32) - stat_ref[0:1]) * stat_ref[1:2]
        return (
            carry[0] + jnp.sum(norm_grad, axis=0, keepdims=True),
            carry[1] + jnp.sum(norm_grad * normed, axis=0, keepdims=True),
        )

    first, second = lax.fori_loop(0, rows, grad_row, (zero, zero))
    cur[2] = jnp.concatenate([first, second], axis=0)
    send_stage(2, plane_peers(f, r), near.at[1])
    cur[3] = end_stage(2, near.at[1])
    send_stage(3, line_peers(f, r), far.at[1])

    @pl.when(f > 0)
    def _():
        def own_sent(p, c):
            own_copy(p).wait_send()
            return c

        lax.fori_loop(8 - ahead, 8, own_sent, 0)

    @pl.when((f == 0) | (f == 2))
    def _():
        def sent(p, c):
            relay_copy(p).wait_send()
            return c

        lax.fori_loop(0, 8, sent, 0)

    def halo_sent(a, c):
        @pl.when(r > 0)
        def _():
            halo_up(a).wait_send()

        @pl.when(r < STRIPS - 1)
        def _():
            halo_down(a).wait_send()
        return c

    lax.fori_loop(0, slots, halo_sent, 0)
    total = over_group(end_stage(3, far.at[1]), channels) / cells_per
    stat_ref[2:4] = total

    def out_row(y, c):
        normed = (xin[y].astype(jnp.float32) - stat_ref[0:1]) * stat_ref[1:2]
        input_grad = stat_ref[1:2] * (slope[y] - stat_ref[2:3] - normed * stat_ref[3:4])
        out_ref[0, y] = input_grad.astype(jnp.bfloat16)
        return c

    lax.fori_loop(0, rows, out_row, 0)
    for k, slots_ref in enumerate((near.at[0], far.at[0], near.at[1], far.at[1])):
        whole_stage(k, slots_ref).wait_send()


def shards(inputs, cotangent, kernel, norm_gain, norm_bias):
    _, rows, width, channels = inputs.shape
    cells_per = FRAMES * STRIPS * rows * width * (channels // GROUPS)
    vmem, anywhere = pl.BlockSpec(memory_space=pltpu.VMEM), pl.BlockSpec(memory_space=pltpu.HBM)
    dma = pltpu.SemaphoreType.DMA
    return pl.pallas_call(
        functools.partial(body, cells_per),
        out_shape=jax.ShapeDtypeStruct(inputs.shape, jnp.bfloat16),
        in_specs=[anywhere] * 5,
        out_specs=vmem,
        scratch_shapes=[
            pltpu.VMEM((4, channels), jnp.float32),
            pltpu.VMEM((rows, width, channels), jnp.bfloat16),
            pltpu.VMEM((1, channels), jnp.float32),
            pltpu.VMEM((1, channels), jnp.float32),
            pltpu.VMEM((rows, width, channels), jnp.bfloat16),
            pltpu.VMEM((3, rows + 2, 2, width, channels // 2), jnp.bfloat16),
            pltpu.VMEM((3, 3, 3 * channels, channels), jnp.bfloat16),
            pltpu.VMEM((rows, width + 2 * PAD, 3 * channels), jnp.float32),
            pltpu.VMEM((rows, width, channels), jnp.float32),
            pltpu.VMEM((4, 2, channels), jnp.float32),
            pltpu.VMEM((2, 15, 2, channels), jnp.float32),
            pltpu.VMEM((2, 15, 2, channels), jnp.float32),
            dma((5,)), dma((3,)), dma((8,)), dma((2, 8)), dma((8,)),
            dma((3, 2)), dma((3, 2)), dma((4,)), dma((4,)),
        ],
        compiler_params=pltpu.CompilerParams(
            collective_id=0, has_side_effects=True, vmem_limit_bytes=61 << 20
        ),
    )(
        inputs, cotangent, kernel.reshape(3, 3, 3 * channels, channels),
        norm_gain[None], norm_bias[None],
    )


def solution(mesh):
    placed = P("frames", "rows", None, None)
    return jax.shard_map(
        shards, mesh=mesh, in_specs=(placed, placed, P(), P(), P()), out_specs=placed, check_vma=False
    )
```
